32 devices in a mesh: inter: 8 (over y, x, core), intra: 4 (over z).
Axes of the slice: x: 2, y: 2, z: 4, core: 2. Of those that a mesh axis runs over, the one named last changes fastest.
Arguments:
- layer_input: bfloat16 [6144, 3584], P(('inter', 'intra')), may hold values from -6 to 6
- up_cotangent: bfloat16 [6144, 10240], P(('inter', 'intra')), may hold values from -6 to 6
- master: float32 [10240, 3584], P(('intra', 'inter')), may hold values from -0.6 to 0.6
- first_moment: float32 [10240, 3584], P(('intra', 'inter')), may hold values from -6 to 6
- second_moment: float32 [10240, 3584], P(('intra', 'inter')), may hold values from 0.2 to 0.5
Outputs:
- new_master: float32 [10240, 3584], P(('intra', 'inter'))
- new_first: float32 [10240, 3584], P(('intra', 'inter'))
- new_second: float32 [10240, 3584], P(('intra', 'inter'))
- new_copy: bfloat16 [10240, 3584], P('intra')
The draws below stay inside these ranges and needn't reach their ends.
All inputs are finite; a program needn't handle non-finite values.
Results may differ from the reference program's by a relative error of at most 0.015.
Values may be sent and summed in bfloat16 or wider, within the bound.
A program may use at most 192 MiB of HBM per device.

```python
import math
import jax
import jax.numpy as jnp
from jax import lax

COLS = 3584
BUCKET = 10240
TOKENS = 6144


def spiked(values, own_key, source, target, shards_of, factor):
    def block_of(position):
        return (jnp.arange(values.shape[position]) // (values.shape[position] // shards_of)).reshape((-1,) + (1,) * (values.ndim - 1 - position))

    near = jax.random.permutation(own_key, shards_of)[block_of(target)]
    other_side = (block_of(target) + shards_of // 2) % shards_of
    return jnp.where((block_of(source) == near) | (block_of(source) == other_side), factor * values, values)


def level_of(key, dims, shards, smallest, largest):
    factor_of, own = 1.0, jax.random.fold_in(key, 6)
    for dim, shards_of in shards:
        heights = jnp.exp(jax.random.uniform(jax.random.fold_in(own, dim), (shards_of,), jnp.float32, smallest / len(shards), largest / len(shards)))
        factor_of = factor_of * jnp.repeat(heights, dims[dim] // shards_of).reshape([-1 if axis == dim else 1 for axis in range(len(dims))])
    return factor_of


def centred(stream_key, shape, deviation, bound, shards=(), kind=jnp.bfloat16):
    array = deviation * jax.random.normal(stream_key, shape, jnp.float32)
    if shards:
        array = array * level_of(stream_key, shape, shards, -0.22, 0.18)
    return jnp.clip(array, -bound, bound).astype(kind)


def gaussian_with(stream_key, shape, scale, reach, split, heavy, held_as=jnp.bfloat16):
    result = scale * jax.random.normal(stream_key, shape, jnp.float32)
    if split:
        result = result * level_of(stream_key, shape, split, -0.22, 0.18)
    return jnp.clip(spiked(result, jax.random.fold_in(stream_key, 3), *heavy), -reach, reach).astype(held_as)


def setup_inputs(seed: int = 0) -> dict:
    key_list = jax.random.split(jax.random.key(seed), 6)
    return {
        "layer_input": centred(key_list[0], (TOKENS, COLS), 1.0, 6.0, ((0, 32),)),
        "up_cotangent": gaussian_with(key_list[1], (TOKENS, BUCKET), 1.0, 6.0, ((0, 32),), (0, 1, 32, 2.75)),
        "master": centred(key_list[2], (BUCKET, COLS), 0.1, 0.6, ((0, 32),), jnp.float32),
        "first_moment": centred(key_list[3], (BUCKET, COLS), 1.0, 6.0, ((0, 32),), jnp.float32),
        "second_moment": jnp.clip(jnp.exp(math.log(0.5) - 0.9162907 * jax.random.uniform(key_list[4], (BUCKET, COLS), jnp.float32) ** level_of(key_list[4], (BUCKET, COLS), ((0, 32),), -0.2, 0.2)), 0.2, 0.5),
    }


def adamw(grad, master, first_moment, second_moment):
    new_first = 0.9 * first_moment + 0.1 * grad
    new_second = 0.95 * second_moment + 0.05 * (grad * grad)
    first_hat = new_first / (1.0 - 0.9 ** 10)
    second_hat = new_second / (1.0 - 0.95 ** 10)
    step_dir = first_hat / (jnp.sqrt(second_hat) + 1e-08) + 0.1 * master
    new_master = master - 0.02 * step_dir
    return (new_master, new_first, new_second)

def reference(layer_input, up_cotangent, master, first_moment, second_moment):
    summed = lax.dot_general(up_cotangent, layer_input, (((0,), (0,)), ((), ())), preferred_element_type=jnp.float32)
    grad = summed * (1.0 / math.sqrt(TOKENS))
    new_master, new_first, new_second = adamw(grad, master, first_moment, second_moment)
    new_copy = new_master.astype(jnp.bfloat16)
    return (new_master, new_first, new_second, new_copy)
```

```python
import functools
import math

import jax
import jax.numpy as jnp
from jax import lax
from jax.experimental import pallas as pl
from jax.experimental.pallas import tpu as pltpu
from jax.sharding import PartitionSpec as P

MESH = pl.DeviceIdType.MESH
STEP = 16


def kernel(
    n, m, group, parts,
    x_ref, cot_ref, m_in, f_in, s_in,
    m_out, f_out, s_out, c_out,
    xg, cg, tr, outb, mine, sib, rs, mbuf, fbuf, sbuf, cbuf,
    x_local, x_send, x_recv, c_local, c_send, c_recv, sib_send, sib_recv,
    rs_send, rs_recv, in_sem, out_sem, ag_send, ag_recv, own_sem, fw_send, fw_recv,
):
    i = lax.axis_index("inter")
    j = lax.axis_index("intra")
    tok, cols = x_ref.shape
    rows = m_in.shape[0]
    nc = m // 2
    core = lax.rem(i, 2)
    chip = i // 2
    other = 1 - core
    sibling = {"inter": chip * 2 + other}
    width = group * 2 * rows
    per_intra = m * rows
    pieces = rows // parts
    scale = 1.0 / math.sqrt(tok * n * m)

    def same_core(c):
        return {"inter": c * 2 + core}

    barrier = pltpu.get_barrier_semaphore()
    for d in range(1, n):
        pl.semaphore_signal(barrier, inc=1, device_id={"intra": lax.rem(j + d, n)}, device_id_type=MESH)
    pl.semaphore_signal(barrier, inc=1, device_id=sibling, device_id_type=MESH)
    for d in range(1, nc):
        pl.semaphore_signal(barrier, inc=1, device_id=same_core(lax.rem(chip + d, nc)), device_id_type=MESH)
    pl.semaphore_wait(barrier, n - 1 + 1 + nc - 1)

    def x_slot(s):
        return xg.at[pl.ds(pl.multiple_of(s * tok, tok), tok), :]

    def x_copy(way, t):
        s = j - t if way == 0 else j + t
        to = j + 1 if way == 0 else j - 1
        return pltpu.make_async_remote_copy(
            src_ref=x_ref if t == 0 else x_slot(s), dst_ref=x_slot(s),
            send_sem=x_send.at[way, t], recv_sem=x_recv.at[way, t],
            device_id={"intra": to}, device_id_type=MESH)

    def x_sends(way, t):
        if way == 0:
            return jnp.logical_and(j - t >= 0, j + 1 < n)
        return jnp.logical_and(j + t < n, j >= 1)

    def x_gets(way, t):
        if way == 0:
            return j - 1 - t >= 0
        return j + 1 + t < n

    def x_arrival(way, t):
        s = j - 1 - t if way == 0 else j + 1 + t
        return pltpu.make_async_remote_copy(
            src_ref=x_slot(s), dst_ref=x_slot(s),
            send_sem=x_send.at[way, t], recv_sem=x_recv.at[way, t],
            device_id={"intra": lax.rem(j + 1, n)}, device_id_type=MESH)

    def part_of(t):
        return lax.rem(chip // group + 1 + t, nc // group)

    def cot_copy(t, d):
        to = lax.rem(j + d, n)
        start = pl.multiple_of(to * per_intra + part_of(t) * width, 128)
        return pltpu.make_async_remote_copy(
            src_ref=cot_ref.at[:, pl.ds(start, width)],
            dst_ref=cg.at[t, pl.ds(pl.multiple_of(j * tok, tok), tok), :],
            send_sem=c_send.at[t, d - 1], recv_sem=c_recv.at[t, d - 1],
            device_id={"intra": to}, device_id_type=MESH)

    def cot_local(t):
        start = pl.multiple_of(j * per_intra + part_of(t) * width, 128)
        return pltpu.make_async_copy(
            cot_ref.at[:, pl.ds(start, width)],
            cg.at[t, pl.ds(pl.multiple_of(j * tok, tok), tok), :],
            c_local.at[t])

    for way in range(2):
        @pl.when(x_sends(way, 0))
        def _():
            x_copy(way, 0).start()
    own_x = pltpu.make_async_copy(x_ref, x_slot(j), x_local)
    own_x.start()
    state = [(m_in, mbuf), (f_in, fbuf), (s_in, sbuf)]
    for t in range(nc // group):
        cot_local(t).start()
    for t in range(1, n):
        for way in range(2):
            @pl.when(x_gets(way, t - 1))
            def _():
                x_arrival(way, t - 1).wait_recv()
            if t < n - 1:
                @pl.when(x_sends(way, t))
                def _():
                    x_copy(way, t).start()
        if t == max(n - 2, 1):
            for s in range(nc // group):
                for d in range(1, n):
                    cot_copy(s, d).start()
    for k, (src, dst) in enumerate(state):
        pltpu.make_async_copy(src, dst, in_sem.at[k]).start()
    own_x.wait()

    tile = 512 if cols % 512 == 0 else 128

    def product(dst, off):
        @pl.loop(0, cols // tile)
        def _(k):
            c0 = pl.multiple_of(k * tile, tile)
            dst[:, pl.ds(c0, tile)] = jnp.dot(
                tr[pl.ds(pl.multiple_of(off, 16), rows), :], xg[:, pl.ds(c0, tile)],
                preferred_element_type=jnp.float32).astype(jnp.bfloat16)

    def sib_copy(e):
        return pltpu.make_async_remote_copy(
            src_ref=outb.at[e % 2], dst_ref=sib.at[e],
            send_sem=sib_send.at[e], recv_sem=sib_recv.at[e],
            device_id=sibling, device_id_type=MESH)

    def rs_copy(e, q, d):
        return pltpu.make_async_remote_copy(
            src_ref=mine.at[e], dst_ref=rs.at[d - 1],
            send_sem=rs_send.at[d - 1], recv_sem=rs_recv.at[d - 1],
            device_id=same_core(q), device_id_type=MESH)

    for t in range(nc // group):
        cot_local(t).wait()
        for d in range(1, n):
            cot_copy(t, d).wait_recv()
        tr[...] = cg[t].T
        for u in range(group):
            e = t * group + u
            if e >= 2:
                sib_copy(e - 2).wait_send()
            product(outb.at[e % 2], (2 * u + other) * rows)
            sib_copy(e).start()
            product(mine.at[e], (2 * u + core) * rows)
            sib_copy(e).wait_recv()
            q = part_of(t) * group + u
            d = lax.rem(q - chip + nc, nc)

            @pl.loop(0, rows // STEP)
            def _(k):
                at = pl.ds(pl.multiple_of(k * STEP, STEP), STEP)
                mine[e, at, :] = (mine[e, at, :].astype(jnp.float32) + sib[e, at, :].astype(jnp.float32)).astype(jnp.bfloat16)

            @pl.when(d != 0)
            def _():
                rs_copy(e, q, d).start()

    for k, (src, dst) in enumerate(state):
        pltpu.make_async_copy(src, dst, in_sem.at[k]).wait()
    last = (nc // group - 1) * group + lax.rem(chip, group)
    for d in range(1, nc):
        rs_copy(0, lax.rem(chip + d, nc), d).wait_recv()

    def out_rows(owner, r):
        return c_out.at[pl.ds(pl.multiple_of(owner * rows + r * pieces, 16), pieces), :]

    def ag_copy(r, d):
        to = sibling if d == 0 else same_core(lax.rem(chip + d, nc))
        return pltpu.make_async_remote_copy(
            src_ref=cbuf.at[pl.ds(r * pieces, pieces), :], dst_ref=out_rows(i, r),
            send_sem=ag_send.at[r, d], recv_sem=ag_recv.at[r, d],
            device_id=to, device_id_type=MESH)

    def forward(r, d):
        from_chip = lax.rem(chip - d + nc, nc)
        ref = out_rows(from_chip * 2 + core, r)
        return pltpu.make_async_remote_copy(
            src_ref=ref, dst_ref=ref,
            send_sem=fw_send.at[r, d - 1], recv_sem=fw_recv.at[r, d - 1],
            device_id=sibling, device_id_type=MESH)

    def own_copy(r):
        return pltpu.make_async_copy(cbuf.at[pl.ds(r * pieces, pieces), :], out_rows(i, r), own_sem.at[r])

    def state_out(r, k):
        src = (mbuf, fbuf, sbuf)[k].at[pl.ds(r * pieces, pieces), :]
        dst = (m_out, f_out, s_out)[k].at[pl.ds(r * pieces, pieces), :]
        return pltpu.make_async_copy(src, dst, out_sem.at[r, k])

    for r in range(parts):
        @pl.loop(0, pieces // STEP)
        def _(k):
            at = pl.ds(pl.multiple_of(r * pieces + k * STEP, STEP), STEP)
            total = mine[last, at, :].astype(jnp.float32)
            for d in range(nc - 1):
                total = total + rs[d, at, :].astype(jnp.float32)
            grad = total * scale
            master = mbuf[at, :]
            new_first = 0.9 * fbuf[at, :] + 0.1 * grad
            new_second = 0.95 * sbuf[at, :] + 0.05 * (grad * grad)
            first_hat = new_first / (1.0 - 0.9**10)
            second_hat = new_second / (1.0 - 0.95**10)
            step_dir = first_hat / (jnp.sqrt(second_hat) + 1e-08) + 0.1 * master
            new_master = master - 0.02 * step_dir
            mbuf[at, :] = new_master
            fbuf[at, :] = new_first
            sbuf[at, :] = new_second
            cbuf[at, :] = new_master.astype(jnp.bfloat16)

        for d in (*range(1, nc), 0):
            ag_copy(r, d).start()
        own_copy(r).start()
        for k in range(3):
            state_out(r, k).start()

    for r in range(parts):
        for d in range(1, nc):
            ag_copy(r, d).wait_recv()
            forward(r, d).start()
    for r in range(parts):
        ag_copy(r, 0).wait_recv()
        own_copy(r).wait()
        for k in range(3):
            state_out(r, k).wait()
        for d in range(1, nc):
            forward(r, d).wait_recv()
            forward(r, d).wait_send()
        for d in range(nc):
            ag_copy(r, d).wait_send()
    for way in range(2):
        for t in range(n - 1):
            @pl.when(x_sends(way, t))
            def _():
                x_copy(way, t).wait_send()
    for t in range(nc // group):
        for d in range(1, n):
            cot_copy(t, d).wait_send()
    for e in range(max(nc - 2, 0), nc):
        sib_copy(e).wait_send()
    for d in range(1, nc):
        rs_copy(0, lax.rem(chip + d, nc), d).wait_send()


def body(n, m, layer_input, up_cotangent, master, first_moment, second_moment):
    tok, cols = layer_input.shape
    rows = master.shape[0]
    nc = m // 2
    group = 1
    while (group * 2 * rows) % 128:
        group *= 2
    count = nc // group
    parts = 5
    bf, f32 = jnp.bfloat16, jnp.float32
    dma = pltpu.SemaphoreType.DMA
    state = jax.ShapeDtypeStruct((rows, cols), f32)
    return pl.pallas_call(
        functools.partial(kernel, n, m, group, parts),
        out_shape=(state, state, state, jax.ShapeDtypeStruct((m * rows, cols), bf)),
        in_specs=[pl.BlockSpec(memory_space=pl.ANY)] * 5,
        out_specs=[pl.BlockSpec(memory_space=pl.ANY)] * 4,
        scratch_shapes=[
            pltpu.VMEM((n * tok, cols), bf),
            pltpu.VMEM((count, n * tok, group * 2 * rows), bf),
            pltpu.VMEM((group * 2 * rows, n * tok), bf),
            pltpu.VMEM((2, rows, cols), bf),
            pltpu.VMEM((nc, rows, cols), bf),
            pltpu.VMEM((nc, rows, cols), bf),
            pltpu.VMEM((nc - 1, rows, cols), bf),
            pltpu.VMEM((rows, cols), f32),
            pltpu.VMEM((rows, cols), f32),
            pltpu.VMEM((rows, cols), f32),
            pltpu.VMEM((rows, cols), bf),
            dma, dma((2, n)), dma((2, n)),
            dma((count,)), dma((count, n - 1)), dma((count, n - 1)),
            dma((nc,)), dma((nc,)),
            dma((nc - 1,)), dma((nc - 1,)),
            dma((3,)), dma((parts, 3)),
            dma((parts, nc)), dma((parts, nc)),
            dma((parts,)),
            dma((parts, nc - 1)), dma((parts, nc - 1)),
        ],
        compiler_params=pltpu.CompilerParams(
            collective_id=0, has_side_effects=True, vmem_limit_bytes=60 * 1024 * 1024),
        cost_estimate=pl.CostEstimate(
            flops=2 * n * tok * m * rows * cols, bytes_accessed=60_000_000, transcendentals=rows * cols),
    )(layer_input, up_cotangent, master, first_moment, second_moment)


def solution(mesh):
    split = P(("inter", "intra"), None)
    owned = P(("intra", "inter"), None)
    return jax.shard_map(
        functools.partial(body, mesh.shape["intra"], mesh.shape["inter"]), mesh=mesh,
        in_specs=(split, split, owned, owned, owned),
        out_specs=(owned, owned, owned, P("intra", None)), check_vma=False)
```

```python
import functools
import math

import jax
import jax.numpy as jnp
from jax import lax
from jax.experimental import pallas as pl
from jax.experimental.pallas import tpu as pltpu
from jax.sharding import PartitionSpec as P

MESH = pl.DeviceIdType.MESH
STEP = 16


def kernel(
    n, m, group, parts, blocks,
    x_ref, cot_ref, m_in, f_in, s_in,
    m_out, f_out, s_out, c_out,
    xg, cg, tr, outb, mine, sib, rs, mbuf, fbuf, sbuf, cbuf,
    x_local, x_send, x_recv, c_local, c_send, c_recv, sib_send, sib_recv,
    rs_send, rs_recv, in_sem, out_sem, ag_send, ag_recv, own_sem, fw_send, fw_recv,
):
    i = lax.axis_index("inter")
    j = lax.axis_index("intra")
    tok, cols = x_ref.shape
    rows = m_in.shape[0]
    nc = m // 2
    core = lax.rem(i, 2)
    chip = i // 2
    other = 1 - core
    sibling = {"inter": chip * 2 + other}
    width = group * 2 * rows
    per_intra = m * rows
    pieces = rows // parts
    scale = 1.0 / math.sqrt(tok * n * m)

    def same_core(c):
        return {"inter": c * 2 + core}

    barrier = pltpu.get_barrier_semaphore()
    for d in range(1, n):
        pl.semaphore_signal(barrier, inc=1, device_id={"intra": lax.rem(j + d, n)}, device_id_type=MESH)
    pl.semaphore_signal(barrier, inc=1, device_id=sibling, device_id_type=MESH)
    for d in range(1, nc):
        pl.semaphore_signal(barrier, inc=1, device_id=same_core(lax.rem(chip + d, nc)), device_id_type=MESH)
    pl.semaphore_wait(barrier, n - 1 + 1 + nc - 1)

    def at_cols(h):
        return pl.ds(*blocks[h])

    def x_slot(s, h):
        return xg.at[pl.ds(pl.multiple_of(s * tok, tok), tok), at_cols(h)]

    def x_copy(h, way, t):
        s = j - t if way == 0 else j + t
        to = j + 1 if way == 0 else j - 1
        return pltpu.make_async_remote_copy(
            src_ref=x_ref.at[:, at_cols(h)] if t == 0 else x_slot(s, h), dst_ref=x_slot(s, h),
            send_sem=x_send.at[h, way, t], recv_sem=x_recv.at[h, way, t],
            device_id={"intra": to}, device_id_type=MESH)

    def x_sends(way, t):
        if way == 0:
            return jnp.logical_and(j - t >= 0, j + 1 < n)
        return jnp.logical_and(j + t < n, j >= 1)

    def x_gets(way, t):
        if way == 0:
            return j - 1 - t >= 0
        return j + 1 + t < n

    def x_arrival(h, way, t):
        s = j - 1 - t if way == 0 else j + 1 + t
        return pltpu.make_async_remote_copy(
            src_ref=x_slot(s, h), dst_ref=x_slot(s, h),
            send_sem=x_send.at[h, way, t], recv_sem=x_recv.at[h, way, t],
            device_id={"intra": lax.rem(j + 1, n)}, device_id_type=MESH)

    def part_of(t):
        return lax.rem(chip // group + 1 + t, nc // group)

    def cot_copy(t, d):
        to = lax.rem(j + d, n)
        start = pl.multiple_of(to * per_intra + part_of(t) * width, 128)
        return pltpu.make_async_remote_copy(
            src_ref=cot_ref.at[:, pl.ds(start, width)],
            dst_ref=cg.at[t, pl.ds(pl.multiple_of(j * tok, tok), tok), :],
            send_sem=c_send.at[t, d - 1], recv_sem=c_recv.at[t, d - 1],
            device_id={"intra": to}, device_id_type=MESH)

    def cot_local(t):
        start = pl.multiple_of(j * per_intra + part_of(t) * width, 128)
        return pltpu.make_async_copy(
            cot_ref.at[:, pl.ds(start, width)],
            cg.at[t, pl.ds(pl.multiple_of(j * tok, tok), tok), :],
            c_local.at[t])

    def x_begin(h):
        for way in range(2):
            @pl.when(x_sends(way, 0))
            def _():
                x_copy(h, way, 0).start()

    def x_relay(h, t):
        for way in range(2):
            @pl.when(x_gets(way, t - 1))
            def _():
                x_arrival(h, way, t - 1).wait_recv()
            if t < n - 1:
                @pl.when(x_sends(way, t))
                def _():
                    x_copy(h, way, t).start()

    x_begin(0)
    own_x = pltpu.make_async_copy(x_ref, xg.at[pl.ds(pl.multiple_of(j * tok, tok), tok), :], x_local)
    own_x.start()
    state = [(m_in, mbuf), (f_in, fbuf), (s_in, sbuf)]
    for t in range(nc // group):
        cot_local(t).start()
    for t in range(1, n):
        x_relay(0, t)
        if t == max(n - 2, 1):
            for s in range(nc // group):
                for d in range(1, n):
                    cot_copy(s, d).start()
    for k, (src, dst) in enumerate(state):
        pltpu.make_async_copy(src, dst, in_sem.at[k]).start()
    own_x.wait()

    def product(dst, h, off):
        start, size = blocks[h]
        tile = 512 if size % 512 == 0 else 128

        @pl.loop(0, size // tile)
        def _(k):
            c0 = pl.multiple_of(start + k * tile, 128)
            dst[:, pl.ds(c0, tile)] = jnp.dot(
                tr[pl.ds(pl.multiple_of(off, 16), rows), :], xg[:, pl.ds(c0, tile)],
                preferred_element_type=jnp.float32).astype(jnp.bfloat16)

    def sib_copy(h, e):
        return pltpu.make_async_remote_copy(
            src_ref=outb.at[e % 2, :, at_cols(h)], dst_ref=sib.at[e, :, at_cols(h)],
            send_sem=sib_send.at[h, e], recv_sem=sib_recv.at[h, e],
            device_id=sibling, device_id_type=MESH)

    def rs_copy(h, e, q, d):
        return pltpu.make_async_remote_copy(
            src_ref=mine.at[e, :, at_cols(h)], dst_ref=rs.at[d - 1, :, at_cols(h)],
            send_sem=rs_send.at[h, d - 1], recv_sem=rs_recv.at[h, d - 1],
            device_id=same_core(q), device_id_type=MESH)

    def part_sums(h, t):
        tr[...] = cg[t].T
        for u in range(group):
            e = t * group + u
            if e >= 2:
                sib_copy(h, e - 2).wait_send()
            product(outb.at[e % 2], h, (2 * u + other) * rows)
            sib_copy(h, e).start()
            product(mine.at[e], h, (2 * u + core) * rows)
            sib_copy(h, e).wait_recv()
            q = part_of(t) * group + u
            d = lax.rem(q - chip + nc, nc)

            @pl.loop(0, rows // STEP)
            def _(k):
                at = pl.ds(pl.multiple_of(k * STEP, STEP), STEP)
                mine[e, at, at_cols(h)] = (
                    mine[e, at, at_cols(h)].astype(jnp.float32) + sib[e, at, at_cols(h)].astype(jnp.float32)
                ).astype(jnp.bfloat16)

            @pl.when(d != 0)
            def _():
                rs_copy(h, e, q, d).start()

    last = (nc // group - 1) * group + lax.rem(chip, group)

    def out_rows(h, owner, r):
        return c_out.at[pl.ds(pl.multiple_of(owner * rows + r * pieces, 16), pieces), at_cols(h)]

    def ag_copy(h, r, d):
        to = sibling if d == 0 else same_core(lax.rem(chip + d, nc))
        return pltpu.make_async_remote_copy(
            src_ref=cbuf.at[pl.ds(r * pieces, pieces), at_cols(h)], dst_ref=out_rows(h, i, r),
            send_sem=ag_send.at[h, r, d], recv_sem=ag_recv.at[h, r, d],
            device_id=to, device_id_type=MESH)

    def forward(h, r, d):
        from_chip = lax.rem(chip - d + nc, nc)
        ref = out_rows(h, from_chip * 2 + core, r)
        return pltpu.make_async_remote_copy(
            src_ref=ref, dst_ref=ref,
            send_sem=fw_send.at[h, r, d - 1], recv_sem=fw_recv.at[h, r, d - 1],
            device_id=sibling, device_id_type=MESH)

    def own_copy(h, r):
        return pltpu.make_async_copy(
            cbuf.at[pl.ds(r * pieces, pieces), at_cols(h)], out_rows(h, i, r), own_sem.at[h, r])

    def state_out(h, r, k):
        src = (mbuf, fbuf, sbuf)[k].at[pl.ds(r * pieces, pieces), at_cols(h)]
        dst = (m_out, f_out, s_out)[k].at[pl.ds(r * pieces, pieces), at_cols(h)]
        return pltpu.make_async_copy(src, dst, out_sem.at[h, r, k])

    def update(h):
        for d in range(1, nc):
            rs_copy(h, 0, lax.rem(chip + d, nc), d).wait_recv()
        cs = at_cols(h)
        for r in range(parts):
            @pl.loop(0, pieces // STEP)
            def _(k):
                at = pl.ds(pl.multiple_of(r * pieces + k * STEP, STEP), STEP)
                total = mine[last, at, cs].astype(jnp.float32)
                for d in range(nc - 1):
                    total = total + rs[d, at, cs].astype(jnp.float32)
                grad = total * scale
                master = mbuf[at, cs]
                new_first = 0.9 * fbuf[at, cs] + 0.1 * grad
                new_second = 0.95 * sbuf[at, cs] + 0.05 * (grad * grad)
                first_hat = new_first / (1.0 - 0.9**10)
                second_hat = new_second / (1.0 - 0.95**10)
                step_dir = first_hat / (jnp.sqrt(second_hat) + 1e-08) + 0.1 * master
                new_master = master - 0.02 * step_dir
                mbuf[at, cs] = new_master
                fbuf[at, cs] = new_first
                sbuf[at, cs] = new_second
                cbuf[at, cs] = new_master.astype(jnp.bfloat16)

            for d in (*range(1, nc), 0):
                ag_copy(h, r, d).start()
            own_copy(h, r).start()
            for k in range(3):
                state_out(h, r, k).start()

    def forwards(h):
        for r in range(parts):
            for d in range(1, nc):
                ag_copy(h, r, d).wait_recv()
                forward(h, r, d).start()

    def sums_sent(h):
        for e in range(max(nc - 2, 0), nc):
            sib_copy(h, e).wait_send()

    count = nc // group
    for t in range(count):
        cot_local(t).wait()
        for d in range(1, n):
            cot_copy(t, d).wait_recv()
        if t == max(count - 2, 0):
            x_begin(1)
        part_sums(0, t)
    sums_sent(0)
    x_relay(1, 1)
    for k, (src, dst) in enumerate(state):
        pltpu.make_async_copy(src, dst, in_sem.at[k]).wait()
    update(0)
    for t in range(2, n):
        x_relay(1, t)
    for t in range(count):
        part_sums(1, t)
    sums_sent(1)
    forwards(0)
    update(1)
    forwards(1)

    for h in range(len(blocks)):
        for r in range(parts):
            ag_copy(h, r, 0).wait_recv()
            own_copy(h, r).wait()
            for k in range(3):
                state_out(h, r, k).wait()
            for d in range(1, nc):
                forward(h, r, d).wait_recv()
                forward(h, r, d).wait_send()
            for d in range(nc):
                ag_copy(h, r, d).wait_send()
        for way in range(2):
            for t in range(n - 1):
                @pl.when(x_sends(way, t))
                def _():
                    x_copy(h, way, t).wait_send()
        for d in range(1, nc):
            rs_copy(h, 0, lax.rem(chip + d, nc), d).wait_send()
    for t in range(count):
        for d in range(1, n):
            cot_copy(t, d).wait_send()


def body(n, m, layer_input, up_cotangent, master, first_moment, second_moment):
    tok, cols = layer_input.shape
    rows = master.shape[0]
    nc = m // 2
    group = 1
    while (group * 2 * rows) % 128:
        group *= 2
    count = nc // group
    parts = 5
    first = cols // 128 * 4 // 7 * 128
    blocks = ((0, first), (first, cols - first))
    nb = len(blocks)
    bf, f32 = jnp.bfloat16, jnp.float32
    dma = pltpu.SemaphoreType.DMA
    state = jax.ShapeDtypeStruct((rows, cols), f32)
    return pl.pallas_call(
        functools.partial(kernel, n, m, group, parts, blocks),
        out_shape=(state, state, state, jax.ShapeDtypeStruct((m * rows, cols), bf)),
        in_specs=[pl.BlockSpec(memory_space=pl.ANY)] * 5,
        out_specs=[pl.BlockSpec(memory_space=pl.ANY)] * 4,
        scratch_shapes=[
            pltpu.VMEM((n * tok, cols), bf),
            pltpu.VMEM((count, n * tok, group * 2 * rows), bf),
            pltpu.VMEM((group * 2 * rows, n * tok), bf),
            pltpu.VMEM((2, rows, cols), bf),
            pltpu.VMEM((nc, rows, cols), bf),
            pltpu.VMEM((nc, rows, cols), bf),
            pltpu.VMEM((nc - 1, rows, cols), bf),
            pltpu.VMEM((rows, cols), f32),
            pltpu.VMEM((rows, cols), f32),
            pltpu.VMEM((rows, cols), f32),
            pltpu.VMEM((rows, cols), bf),
            dma, dma((nb, 2, n)), dma((nb, 2, n)),
            dma((count,)), dma((count, n - 1)), dma((count, n - 1)),
            dma((nb, nc)), dma((nb, nc)),
            dma((nb, nc - 1)), dma((nb, nc - 1)),
            dma((3,)), dma((nb, parts, 3)),
            dma((nb, parts, nc)), dma((nb, parts, nc)),
            dma((nb, parts)),
            dma((nb, parts, nc - 1)), dma((nb, parts, nc - 1)),
        ],
        compiler_params=pltpu.CompilerParams(
            collective_id=0, has_side_effects=True, vmem_limit_bytes=60 * 1024 * 1024),
        cost_estimate=pl.CostEstimate(
            flops=2 * n * tok * m * rows * cols, bytes_accessed=60_000_000, transcendentals=rows * cols),
    )(layer_input, up_cotangent, master, first_moment, second_moment)


def solution(mesh):
    split = P(("inter", "intra"), None)
    owned = P(("intra", "inter"), None)
    return jax.shard_map(
        functools.partial(body, mesh.shape["intra"], mesh.shape["inter"]), mesh=mesh,
        in_specs=(split, split, owned, owned, owned),
        out_specs=(owned, owned, owned, P("intra", None)), check_vma=False)
```
